32 devices in a mesh: node: 8 (over y, x, core), batch: 4 (over z).
Axes of the slice: x: 2, y: 2, z: 4, core: 2. Of those that a mesh axis runs over, the one named last changes fastest.
Arguments:
- memory: bfloat16 [65536, 128], P('node'), may hold values from -5 to 5
- src_owner: int32 [16384, 1], P(('node', 'batch')), may hold values from 0 to 7; in each aligned block of 512 rows (0 to 511, 512 to 1023, ...) at most 128 rows name the same one
- src_row: int32 [16384], P(('node', 'batch')), may hold values from 0 to 8191
- fetch_owner: int32 [16384, 11, 1], P(('node', 'batch')), may hold values from 0 to 7; in each aligned block of 5632 rows (0 to 5631, 5632 to 11263, ..., all dimensions but the last counted through in order) at most 1408 rows name the same one
- fetch_row: int32 [16384, 11], P(('node', 'batch')), may hold values from 0 to 8191
- event_tick: int32 [16384], P(('node', 'batch')), may hold values from 5000 to 9999
- source_tick: int32 [16384], P(('node', 'batch')), may hold values from 0 to 4999
- neighbour_tick: int32 [16384, 10], P(('node', 'batch')), may hold values from 0 to 4999
- time_freq: float32 [128], replicated, may hold values from 0.0001 to 0.1
- time_phase: float32 [128], replicated, may hold values from -3.140625 to 3.140625
- gru_input: bfloat16 [256, 384], replicated, may hold values from -0.375 to 0.375
- gru_hidden: bfloat16 [128, 384], replicated, may hold values from -0.5 to 0.5
- gru_bias: float32 [512], replicated, may hold values from -3 to 3
- w_query: bfloat16 [128, 128], replicated, may hold values from -0.5 to 0.5
- w_kv: bfloat16 [256, 256], replicated, may hold values from -0.375 to 0.375
- w_merge: bfloat16 [256, 128], replicated, may hold values from -0.375 to 0.375
- merge_bias: float32 [128], replicated, may hold values from -3 to 3
- out_grad: float32 [16384, 128], P(('node', 'batch')), may hold values from -0.02 to 0.02
Outputs:
- embedding: float32 [16384, 128], P(('node', 'batch'))
- memory_out: bfloat16 [65536, 128], P('node')
- grad_query: float32 [128, 128], replicated
- grad_kv: float32 [256, 256], replicated
- grad_merge: float32 [256, 128], replicated
- grad_bias: float32 [128], replicated
The draws below stay inside these ranges and needn't reach their ends.
Inputs may be any that keep to these rules, and one draw needn't show every extreme that they name: `src_owner`: among the 512 events of one device no owner is named by more than 128 of them. `fetch_owner`: among the 512 * (11) entries of one device no owner is named by more than 1408 of them.
All inputs are finite; a program needn't handle non-finite values.
Results may differ from the reference program's by a relative error of at most 0.012.
Values may be sent and summed in bfloat16 or wider, within the bound.
A program may use at most 64 MiB of HBM per device.

```python
import math
import jax
import jax.numpy as jnp
import numpy as np
from jax import lax

MEM = 128
TIME = 128
HEADS = 2
NB = 10
E_DEV = 512
NODE_DEV = 8192
ATT = 128
OWNERS = 8
EVENTS = 16384
NODES = 65536
FETCH_CAP = 1408
MSG_CAP = 128


def set_ends(values, stream_key, smallest, top_value):
    index_at = [jax.random.randint(jax.random.fold_in(stream_key, axis), (), 0, length) for axis, length in enumerate(values.shape)]
    longest = values.shape.index(max(values.shape))
    neighbour = index_at[:longest] + [(index_at[longest] + 1) % values.shape[longest]] + index_at[longest + 1:]
    return values.at[tuple(index_at)].set(smallest).at[tuple(neighbour)].set(top_value)


def level_of(key, extent, cuts, low, largest):
    gain, own = 1.0, jax.random.fold_in(key, 6)
    for dim, shards_of in cuts:
        heights = jnp.exp(jax.random.uniform(jax.random.fold_in(own, dim), (shards_of,), jnp.float32, low / len(cuts), largest / len(cuts)))
        gain = gain * jnp.repeat(heights, extent[dim] // shards_of).reshape([-1 if axis == dim else 1 for axis in range(len(extent))])
    return gain


def rank_bounds(amount, skew):
    portions = [(1 << 20) // math.isqrt(rank ** skew) + 1 for rank in range(1, amount + 1)]
    spread = 1 + sum(portions) // (1 << 30)
    return np.cumsum(np.array([max(1, weight // spread) for weight in portions]))


def ranked(stream_key, dims, number_of, slope):
    table = rank_bounds(number_of, slope)
    ticket = jax.random.randint(jax.random.fold_in(stream_key, 1), dims, 0, int(table[number_of - 1]))
    grade = jnp.searchsorted(jnp.asarray(table, jnp.int32), ticket, side="right")
    return jax.random.permutation(jax.random.fold_in(stream_key, 2), number_of)[grade].astype(jnp.int32)


def shared_out(rng, own, number, rows, amount, top, limit, lean):
    sequence = jax.random.permutation(rng, amount)
    heavy_load, ordinary = portions_of(amount, rows * top, limit, lean, True), portions_of(amount, rows * top, limit, lean, False)
    places = jnp.arange(amount)

    def named(sizes, rotation):
        used = int((sizes > 0).sum())
        fixed = max(1, used // 4)
        shifted = fixed + (places - fixed + rotation * (used - fixed)) % max(1, amount - fixed)
        return jnp.zeros((amount,), jnp.int32).at[sequence[jnp.where(places < fixed, places, shifted)]].set(jnp.asarray(sizes, jnp.int32))

    sizes = jnp.where(number % 4 == 0, named(heavy_load, number // 4), named(ordinary, number - number // 4 - 1))
    mixed = jax.random.permutation(jax.random.fold_in(own, 3), amount)
    source_of, receiver = mixed[0:amount // 2 * 2:2], mixed[1:amount // 2 * 2:2]
    margin = jnp.minimum(sizes[source_of] - 1, limit - sizes[receiver]) // 2
    margin = jnp.where((source_of == sequence[0]) | (receiver == sequence[0]) | (sizes[receiver] == 0), 0, jnp.maximum(margin, 0))
    shifted = jax.random.randint(jax.random.fold_in(own, 4), (amount // 2,), 0, 1 << 20) % (margin + 1)
    sizes = sizes.at[source_of].add(-shifted).at[receiver].add(shifted)
    labels = jnp.searchsorted(jnp.cumsum(sizes), jnp.arange(rows * top), side="right").astype(jnp.int32)
    listing = labels.reshape(top, rows).T
    listing = listing[jax.random.permutation(jax.random.fold_in(own, 1), rows)]
    rotation = jax.random.randint(jax.random.fold_in(own, 2), (rows, 1), 0, top)
    return jnp.take_along_axis(listing, (jnp.arange(top)[None, :] + rotation) % top, axis=1)


def portions_of(count, total, limit, skew, full):
    weights = [(1 << 20) // math.isqrt(standing ** skew) + 1 for standing in range(1, count + 1)]
    largest = limit if full else min(limit, max(-(-total // count), total * weights[0] // sum(weights)))
    least = 1 if total - largest >= count - 1 else 0
    counts, rest = [largest] + [least] * (count - 1), total - largest - least * (count - 1)
    while rest > 0:
        free = [i for i in range(1, count) if counts[i] < largest] or [i for i in range(1, count) if counts[i] < limit]
        whole, budget = sum([weights[i] for i in free]), rest
        for i in free:
            extra = min(limit - counts[i], max(1, budget * weights[i] // whole), rest)
            counts[i] = counts[i] + extra
            rest = rest - extra
    return np.array(counts)


def centred(rng, dims, scale, reach, cuts=(), kind=jnp.bfloat16):
    values = jax.random.normal(rng, dims, jnp.float32) * scale
    if len(cuts) > 0:
        values = level_of(rng, dims, cuts, -0.22, 0.18) * values
    return jnp.clip(values, min=-reach, max=reach).astype(kind)


def setup_inputs(seed: int = 0) -> dict:
    keys = jax.random.split(jax.random.key(seed), 19)
    memory = centred(keys[0], (NODES, MEM), 1.0, 5.0, ((0, 8),))
    src_owner_keys = jax.random.split(jax.random.fold_in(keys[1], 1), EVENTS // E_DEV)
    src_owner_turns = jax.random.permutation(jax.random.fold_in(keys[1], 3), EVENTS // E_DEV)
    src_owner = jax.vmap(lambda own, number: shared_out(jax.random.fold_in(keys[1], 2), own, number, E_DEV, OWNERS, 1, MSG_CAP, 1))(src_owner_keys, src_owner_turns).reshape((EVENTS, 1))
    src_row = set_ends(ranked(keys[2], (EVENTS,), NODE_DEV, 2), jax.random.fold_in(keys[2], 3), 0, NODE_DEV - 1).astype(jnp.int32)
    fetch_owner_keys = jax.random.split(jax.random.fold_in(keys[3], 1), EVENTS * (NB + 1) // (E_DEV * (NB + 1)))
    fetch_owner_turns = jax.random.permutation(jax.random.fold_in(keys[3], 3), EVENTS * (NB + 1) // (E_DEV * (NB + 1)))
    fetch_owner = jax.vmap(lambda own, number: shared_out(jax.random.fold_in(keys[3], 2), own, number, E_DEV * (NB + 1), OWNERS, 1, FETCH_CAP, 1))(fetch_owner_keys, fetch_owner_turns).reshape((EVENTS, NB + 1, 1))
    fetch_row = set_ends(ranked(keys[4], (EVENTS, NB + 1), NODE_DEV, 2), jax.random.fold_in(keys[4], 3), 0, NODE_DEV - 1).astype(jnp.int32)
    event_tick = set_ends(jax.random.randint(keys[5], (EVENTS,), 5000, 10000), jax.random.fold_in(keys[5], 1), 5000, 9999).astype(jnp.int32)
    source_tick = set_ends(jax.random.randint(keys[6], (EVENTS,), 0, 5000), jax.random.fold_in(keys[6], 1), 0, 4999).astype(jnp.int32)
    neighbour_tick = set_ends(jax.random.randint(keys[7], (EVENTS, NB), 0, 5000), jax.random.fold_in(keys[7], 1), 0, 4999).astype(jnp.int32)
    time_freq = jnp.clip(jnp.exp(jax.random.uniform(keys[8], (TIME,), jnp.float32, math.log(0.0001), math.log(0.1))), 0.0001, 0.1)
    time_phase = jnp.clip(jax.random.uniform(keys[9], (TIME,), jnp.float32, -3.140625, 3.140625), -3.140625, 3.140625)
    gru_input = centred(keys[10], (MEM + TIME, 3 * MEM), (MEM + TIME) ** -0.5, 0.375)
    gru_hidden = centred(keys[11], (MEM, 3 * MEM), MEM ** -0.5, 0.5)
    gru_bias = centred(keys[12], (4 * MEM,), 0.5, 3.0, (), jnp.float32)
    w_query = centred(keys[13], (MEM, ATT), MEM ** -0.5, 0.5)
    w_kv = centred(keys[14], (MEM + TIME, 2 * ATT), (MEM + TIME) ** -0.5, 0.375)
    w_merge = centred(keys[15], (ATT + MEM, MEM), (ATT + MEM) ** -0.5, 0.375)
    merge_bias = centred(keys[16], (MEM,), 0.5, 3.0, (), jnp.float32)
    out_grad = centred(keys[17], (EVENTS, MEM), 0.003, 0.02, ((0, 32),), jnp.float32)
    return {"memory": memory, "src_owner": src_owner, "src_row": src_row, "fetch_owner": fetch_owner, "fetch_row": fetch_row, "event_tick": event_tick, "source_tick": source_tick, "neighbour_tick": neighbour_tick, "time_freq": time_freq, "time_phase": time_phase, "gru_input": gru_input, "gru_hidden": gru_hidden, "gru_bias": gru_bias, "w_query": w_query, "w_kv": w_kv, "w_merge": w_merge, "merge_bias": merge_bias, "out_grad": out_grad}


def time_code(delta, freq, phase):
    return jnp.cos(delta[..., None] * freq + phase)

def gru_cell(message, state, gru_input, gru_hidden, gru_bias):
    width = state.shape[-1]
    from_msg = jnp.dot(message, gru_input, preferred_element_type=jnp.float32) + gru_bias[:3 * width]
    from_state = jnp.dot(state, gru_hidden, preferred_element_type=jnp.float32)
    reset = jax.nn.sigmoid(from_msg[:, :width] + from_state[:, :width])
    update = jax.nn.sigmoid(from_msg[:, width:2 * width] + from_state[:, width:2 * width])
    candid = jnp.tanh(from_msg[:, 2 * width:] + reset * (from_state[:, 2 * width:] + gru_bias[3 * width:]))
    return ((1.0 - update) * candid + update * state.astype(jnp.float32)).astype(jnp.bfloat16)

def last_pick(owner_ids, row_ids):
    same = (owner_ids[:, None] == owner_ids[None, :]) & (row_ids[:, None] == row_ids[None, :])
    places = jnp.arange(owner_ids.shape[0], dtype=jnp.int32)
    return lax.optimization_barrier(jnp.max(jnp.where(same, places[None, :], jnp.int32(-1)), axis=1)).astype(jnp.int32)

def embed(query_w, pair_w, merge_w, bias_term, new_src, kv_in):
    att_width = query_w.shape[1]
    head_width = att_width // HEADS
    row_count = new_src.shape[0]
    nb_count = kv_in.shape[1]
    query_rows = jnp.dot(new_src, query_w.astype(jnp.bfloat16), preferred_element_type=jnp.float32)
    pairs = jnp.dot(kv_in, pair_w.astype(jnp.bfloat16), preferred_element_type=jnp.float32)
    key_rows = pairs[..., :att_width].reshape(row_count, nb_count, HEADS, head_width)
    value_rows = pairs[..., att_width:].reshape(row_count, nb_count, HEADS, head_width)
    scores = jnp.einsum('ehd,enhd->ehn', query_rows.reshape(row_count, HEADS, head_width), key_rows) / math.sqrt(head_width)
    scores = scores - lax.optimization_barrier(jnp.max(scores, axis=-1, keepdims=True))
    shares = jnp.exp(scores)
    shares = shares / lax.optimization_barrier(jnp.sum(shares, axis=-1, keepdims=True))
    mixed = jnp.einsum('ehn,enhd->ehd', shares, value_rows).reshape(row_count, att_width).astype(jnp.bfloat16)
    joined = jnp.concatenate([mixed, new_src], axis=-1)
    return jax.nn.silu(jnp.dot(joined, merge_w.astype(jnp.bfloat16), preferred_element_type=jnp.float32) + bias_term)

def reference(memory, src_owner, src_row, fetch_owner, fetch_row, event_tick, source_tick, neighbour_tick, time_freq, time_phase, gru_input, gru_hidden, gru_bias, w_query, w_kv, w_merge, merge_bias, out_grad):
    blocks = src_row.shape[0] // E_DEV

    def split(array):
        return array.reshape((blocks, E_DEV) + array.shape[1:])
    pieces_all = tuple((split(array) for array in (src_owner[:, 0], src_row, fetch_owner[:, :, 0], fetch_row, event_tick, source_tick, neighbour_tick, out_grad)))
    weights_wide = (w_query.astype(jnp.float32), w_kv.astype(jnp.float32), w_merge.astype(jnp.float32), merge_bias)

    def step(carry, pieces):
        totals, written = carry
        owner_ids, row_ids, far_owner, far_row, ticks, src_ticks, nb_ticks, cotang = pieces
        node_ids = (owner_ids * NODE_DEV + row_ids).astype(jnp.int32)
        state = memory[node_ids]
        fetched = memory[(far_owner * NODE_DEV + far_row).astype(jnp.int32)]
        source_code = time_code((ticks - src_ticks).astype(jnp.float32), time_freq, time_phase).astype(jnp.bfloat16)
        message = jnp.concatenate([fetched[:, 0], source_code], axis=-1)
        updated = gru_cell(message, state, gru_input, gru_hidden, gru_bias)
        new_src = updated[last_pick(owner_ids, row_ids)]
        written = written.at[node_ids].set(new_src)
        nb_code = time_code((ticks[:, None] - nb_ticks).astype(jnp.float32), time_freq, time_phase).astype(jnp.bfloat16)
        kv_in = jnp.concatenate([fetched[:, 1:], nb_code], axis=-1)

        def forward(query_w, pair_w, merge_w, bias_term):
            return embed(query_w, pair_w, merge_w, bias_term, new_src, kv_in)
        result, pull = jax.vjp(forward, *weights_wide)
        grads = pull(cotang)
        return ((tuple((total + part for total, part in zip(totals, grads))), written), result)
    zeros = tuple((jnp.zeros_like(weight) for weight in weights_wide))
    (grads, memory_out), results = lax.scan(step, (zeros, memory), pieces_all)
    return (results.reshape(-1, results.shape[-1]), memory_out, grads[0], grads[1], grads[2], grads[3])
```

```python
import functools
import math

import jax
import jax.numpy as jnp
from jax import lax
from jax.experimental import pallas as pl
from jax.experimental.pallas import tpu as pltpu
from jax.sharding import PartitionSpec as P

HEADS = 2
LANES = 128
F32 = jnp.float32
BF16 = jnp.bfloat16
VMEM = pltpu.VMEM
SMEM = pltpu.SMEM
COS_TERMS = [(-1.0) ** k * (2 * math.pi) ** (2 * k) / math.factorial(2 * k) for k in range(9)]


def cos_code(delta, freq, phase):
    turns = delta[..., None] * (freq * (0.5 / math.pi)) + phase * (0.5 / math.pi)
    turns = turns - jnp.round(turns)
    square = turns * turns
    total = jnp.full_like(square, COS_TERMS[-1])
    for term in COS_TERMS[-2::-1]:
        total = total * square + term
    return total.astype(BF16)


def ranks(owner_grid, owner_count):
    rows, lanes = owner_grid.shape
    masks = (owner_grid[None] == jnp.arange(owner_count, dtype=jnp.int32)[:, None, None]).astype(BF16)
    lane_before = jnp.triu(jnp.ones((lanes, lanes), BF16), 1)
    row_before = jnp.triu(jnp.ones((rows, rows), BF16), 1)
    within = jnp.einsum("orl,lm->orm", masks, lane_before, preferred_element_type=F32)
    totals = jnp.sum(masks.astype(F32), axis=-1).astype(BF16)
    base = jnp.einsum("or,rs->os", totals, row_before, preferred_element_type=F32)
    return jnp.sum(masks.astype(F32) * (within + base[:, :, None]), axis=0).astype(jnp.int32)


def spread(slot, value, slot_count):
    hi, lo = slot // LANES, slot % LANES
    bump = value + 1
    at_hi = hi[None, :] == jnp.arange(slot_count // LANES, dtype=jnp.int32)[:, None]
    upper = jnp.where(at_hi, (bump // 64).astype(F32)[None, :], 0.0).astype(BF16)
    lower = jnp.where(at_hi, (bump % 64).astype(F32)[None, :], 0.0).astype(BF16)
    at_lo = (lo[None, :] == jnp.arange(LANES, dtype=jnp.int32)[:, None]).astype(BF16)
    both = jnp.einsum(
        "he,le->hl", jnp.concatenate([upper, lower], 0), at_lo, preferred_element_type=F32
    ).astype(jnp.int32)
    half = slot_count // LANES
    return both[:half] * 64 + both[half:]


def widen(src_ref, dst_ref, step):
    @pl.loop(0, src_ref.shape[0] // step)
    def _(i):
        at = pl.ds(pl.multiple_of(i * step, step), step)
        dst_ref[at, :] = src_ref[at, :].astype(dst_ref.dtype)


def gather_kernel(owner_count, cap, index_ref, count_ref, table_ref, out_ref, wide, rows):
    widen(table_ref, wide, 256)

    @pl.loop(0, owner_count)
    def _(o):
        base = pl.multiple_of(o * cap, LANES)
        steps = (count_ref[o] + 15) // 16

        @pl.loop(0, steps)
        def _(i):
            for k in range(16):
                row = index_ref[base + i * 16 + k]
                rows[pl.ds(i * 16 + k, 1), :] = wide[pl.ds(row, 1), :]

        @pl.loop(0, steps)
        def _(i):
            at = pl.multiple_of(i * 16, 16)
            out_ref[pl.ds(pl.multiple_of(base + at, 16), 16), :] = rows[pl.ds(at, 16), :].astype(BF16)


def gather(index, count, table, owner_count, cap):
    return pl.pallas_call(
        functools.partial(gather_kernel, owner_count, cap),
        out_shape=jax.ShapeDtypeStruct((owner_count * cap, table.shape[1]), BF16),
        in_specs=[
            pl.BlockSpec(memory_space=SMEM),
            pl.BlockSpec(memory_space=SMEM),
            pl.BlockSpec(memory_space=VMEM),
        ],
        out_specs=pl.BlockSpec(memory_space=VMEM),
        scratch_shapes=[VMEM(table.shape, F32), VMEM((cap, table.shape[1]), F32)],
        compiler_params=pltpu.CompilerParams(vmem_limit_bytes=40 << 20),
        cost_estimate=pl.CostEstimate(flops=10**6, bytes_accessed=10**7, transcendentals=0),
    )(index, count, table)


def update_kernel(
    events, per_event, slot_ref, got_ref, code_ref, pick_ref, near_ref, gi_ref, gh_ref, bias_ref,
    rows_ref, new_ref, out_ref, wide, held,
):
    width = got_ref.shape[1]
    widen(got_ref, wide, 256)

    @pl.loop(0, slot_ref.shape[0] // 16)
    def _(i):
        for k in range(16):
            at = slot_ref[i * 16 + k]
            held[pl.ds(i * 16 + k, 1), :] = wide[pl.ds(at, 1), :]

    @pl.loop(0, events * (per_event - 1) // 256)
    def _(i):
        at = pl.ds(pl.multiple_of(events + i * 256, 256), 256)
        rows_ref[pl.ds(pl.multiple_of(i * 256, 256), 256), :] = held[at, :].astype(BF16)

    dest = held[:events, :].astype(BF16)
    wide_state = held[events * per_event :, :]
    dot = functools.partial(jnp.dot, preferred_element_type=F32)
    a = dot(dest, gi_ref[:width, :]) + dot(code_ref[...], gi_ref[width:, :]) + bias_ref[:, : 3 * width]
    b = dot(wide_state.astype(BF16), gh_ref[...])
    reset = jax.nn.sigmoid(a[:, :width] + b[:, :width])
    update = jax.nn.sigmoid(a[:, width : 2 * width] + b[:, width : 2 * width])
    cand = jnp.tanh(a[:, 2 * width :] + reset * (b[:, 2 * width :] + bias_ref[:, 3 * width :]))
    updated = ((1.0 - update) * cand + update * wide_state).astype(BF16)
    place = lax.broadcasted_iota(jnp.int32, (events, events), 1)
    chosen = (place == pick_ref[...]).astype(F32).astype(BF16)
    new_ref[...] = dot(chosen, updated).astype(BF16)
    slots = out_ref.shape[0]
    spot = lax.broadcasted_iota(jnp.int32, (slots, events), 0)
    out_ref[...] = dot((spot == near_ref[...]).astype(F32).astype(BF16), updated).astype(BF16)


def update(slot, got, code, pick, near_slot, gru_input, gru_hidden, bias, events, per_event, near_slots):
    width = got.shape[1]
    return pl.pallas_call(
        functools.partial(update_kernel, events, per_event),
        out_shape=(
            jax.ShapeDtypeStruct((events * (per_event - 1), width), BF16),
            jax.ShapeDtypeStruct((events, width), BF16),
            jax.ShapeDtypeStruct((near_slots, width), BF16),
        ),
        in_specs=[pl.BlockSpec(memory_space=SMEM)] + [pl.BlockSpec(memory_space=VMEM)] * 7,
        out_specs=(pl.BlockSpec(memory_space=VMEM),) * 3,
        scratch_shapes=[VMEM(got.shape, F32), VMEM((slot.shape[0], width), F32)],
        compiler_params=pltpu.CompilerParams(vmem_limit_bytes=48 << 20),
        cost_estimate=pl.CostEstimate(flops=10**6, bytes_accessed=10**7, transcendentals=0),
    )(slot, got, code, pick, near_slot, gru_input, gru_hidden, bias)


def attend_kernel(nb, rows_ref, code_ref, new_ref, grad_ref, wq_ref, wkv_ref, wm_ref, mb_ref, emb_ref, out_ref, kv, dkv):
    att = wq_ref.shape[1]
    mem = new_ref.shape[1]
    head = att // HEADS
    scale = 1.0 / math.sqrt(head)
    dot = functools.partial(jnp.dot, preferred_element_type=F32)
    same = (
        lax.broadcasted_iota(jnp.int32, (att, att), 0) // head
        == lax.broadcasted_iota(jnp.int32, (att, att), 1) // head
    ).astype(F32).astype(BF16)

    def head_sum(v):
        upper = v.astype(BF16)
        rest = (v - upper.astype(F32)).astype(BF16)
        return dot(upper, same) + dot(rest, same)

    def over_rows(x, y):
        return lax.dot_general(x, y, (((0,), (0,)), ((), ())), preferred_element_type=F32)

    new = new_ref[...]
    query = dot(new, wq_ref[...])
    scores = []
    for j in range(nb):
        kv[j] = dot(rows_ref[j], wkv_ref[:mem, :]) + dot(code_ref[j], wkv_ref[mem:, :])
        scores.append(head_sum(query * kv[j, :, :att]) * scale)
    top = functools.reduce(jnp.maximum, scores)
    shares = [jnp.exp(s - top) for s in scores]
    inverse = 1.0 / functools.reduce(jnp.add, shares)
    shares = [s * inverse for s in shares]
    mixed = functools.reduce(jnp.add, [shares[j] * kv[j, :, att:] for j in range(nb)]).astype(BF16)
    z = dot(mixed, wm_ref[:att, :]) + dot(new, wm_ref[att:, :]) + mb_ref[...]
    gate = 1.0 / (1.0 + jnp.exp(-z))
    emb_ref[...] = z * gate
    dz = grad_ref[...] * (gate * (1.0 + z * (1.0 - gate)))
    dz16 = dz.astype(BF16)
    dmixed = lax.dot_general(
        dz16, wm_ref[:att, :], (((1,), (1,)), ((), ())), preferred_element_type=F32
    ).astype(BF16).astype(F32)
    dshare = [head_sum(dmixed * kv[j, :, att:]) for j in range(nb)]
    mean = functools.reduce(jnp.add, [shares[j] * dshare[j] for j in range(nb)])
    dquery = jnp.zeros_like(query)
    for j in range(nb):
        dscore = shares[j] * (dshare[j] - mean) * scale
        dquery += dscore * kv[j, :, :att]
        dkv[j, :, :att] = (dscore * query).astype(BF16)
        dkv[j, :, att:] = (shares[j] * dmixed).astype(BF16)
    flat = dkv[...].reshape(-1, 2 * att)
    from_row = over_rows(rows_ref[...].reshape(-1, mem), flat)
    from_code = over_rows(code_ref[...].reshape(-1, code_ref.shape[2]), flat)

    @pl.when(pl.program_id(0) == 0)
    def _():
        out_ref[...] = jnp.zeros_like(out_ref)

    at = 0
    for piece in (
        over_rows(new, dquery.astype(BF16)),
        from_row[:, :att],
        from_code[:, :att],
        from_row[:, att:],
        from_code[:, att:],
        over_rows(mixed, dz16),
        over_rows(new, dz16),
    ):
        out_ref[at : at + piece.shape[0], :] += piece
        at += piece.shape[0]
    out_ref[at : at + 1, :] += jnp.sum(dz, axis=0, keepdims=True)


def attend(rows, code, new, out_grad, wq, wkv, wm, mb, packed_rows, block):
    nb, events, mem = rows.shape
    time = code.shape[2]
    att = wq.shape[1]
    whole = lambda a: pl.BlockSpec(a.shape, lambda i: (0,) * a.ndim)
    return pl.pallas_call(
        functools.partial(attend_kernel, nb),
        grid=(events // block,),
        out_shape=(
            jax.ShapeDtypeStruct(out_grad.shape, F32),
            jax.ShapeDtypeStruct((packed_rows, LANES), F32),
        ),
        in_specs=[
            pl.BlockSpec((nb, block, mem), lambda i: (0, i, 0)),
            pl.BlockSpec((nb, block, time), lambda i: (0, i, 0)),
            pl.BlockSpec((block, mem), lambda i: (i, 0)),
            pl.BlockSpec((block, mem), lambda i: (i, 0)),
            whole(wq),
            whole(wkv),
            whole(wm),
            whole(mb),
        ],
        out_specs=(
            pl.BlockSpec((block, mem), lambda i: (i, 0)),
            pl.BlockSpec((packed_rows, LANES), lambda i: (0, 0)),
        ),
        scratch_shapes=[VMEM((nb, block, 2 * att), F32), VMEM((nb, block, 2 * att), BF16)],
        compiler_params=pltpu.CompilerParams(vmem_limit_bytes=48 << 20),
        cost_estimate=pl.CostEstimate(flops=3 * 10**9, bytes_accessed=10**7, transcendentals=10**6),
    )(rows, code, new, out_grad, wq, wkv, wm, mb)


def write_kernel(senders, batches, cap, row_ref, count_ref, fresh_ref, table_ref, out_ref, wide, rows):
    widen(table_ref, wide, 256)
    widen(fresh_ref, rows, 256)

    @pl.loop(0, senders * batches)
    def _(order):
        block = lax.rem(order, batches) * senders + lax.div(order, batches)
        base = block * cap
        count = count_ref[block]

        @pl.loop(0, lax.div(count, 8))
        def _(i):
            for k in range(8):
                at = base + i * 8 + k
                wide[pl.ds(row_ref[at], 1), :] = rows[pl.ds(at, 1), :]

        @pl.loop(lax.div(count, 8) * 8, count)
        def _(i):
            wide[pl.ds(row_ref[base + i], 1), :] = rows[pl.ds(base + i, 1), :]

    widen(wide, out_ref, 256)


def write_back(row, count, fresh, table, senders, batches, cap):
    return pl.pallas_call(
        functools.partial(write_kernel, senders, batches, cap),
        out_shape=jax.ShapeDtypeStruct(table.shape, BF16),
        in_specs=[
            pl.BlockSpec(memory_space=SMEM),
            pl.BlockSpec(memory_space=SMEM),
            pl.BlockSpec(memory_space=VMEM),
            pl.BlockSpec(memory_space=VMEM),
        ],
        out_specs=pl.BlockSpec(memory_space=VMEM),
        scratch_shapes=[VMEM(table.shape, F32), VMEM(fresh.shape, F32)],
        compiler_params=pltpu.CompilerParams(vmem_limit_bytes=40 << 20),
        cost_estimate=pl.CostEstimate(flops=10**6, bytes_accessed=10**7, transcendentals=0),
    )(row, count, fresh, table)


def on_device(
    memory, src_owner, src_row, fetch_owner, fetch_row, event_tick, source_tick, neighbour_tick,
    time_freq, time_phase, gru_input, gru_hidden, gru_bias, w_query, w_kv, w_merge, merge_bias, out_grad,
):
    owner_count = lax.axis_size("node")
    batch_count = lax.axis_size("batch")
    events = src_row.shape[0]
    per_event = fetch_row.shape[1]
    mem = memory.shape[1]
    att = w_query.shape[1]
    time = time_freq.shape[0]
    near_cap = events * 2 // owner_count
    cap = near_cap * (per_event + 1)
    to_all = functools.partial(lax.all_to_all, axis_name="node", split_axis=0, concat_axis=0, tiled=True)

    near_owner = src_owner[:, 0]
    owners = jnp.concatenate([fetch_owner[:, :, 0].T, near_owner[None]], 0).reshape(-1, LANES)
    wanted = jnp.concatenate([fetch_row.T, src_row[None]], 0).reshape(-1)
    slot = (owners * cap + ranks(owners, owner_count)).reshape(-1)
    ask = spread(slot, wanted, owner_count * cap).reshape(owner_count, cap)
    got = to_all(ask)
    count = jnp.sum((got > 0).astype(jnp.int32), axis=1)
    index = jnp.maximum(got - 1, 0).reshape(-1)
    sent = gather(index, count, memory, owner_count, cap)
    back = to_all(sent.reshape(owner_count, cap, mem)).reshape(-1, mem)

    near_grid = near_owner.reshape(-1, LANES)
    near_slot = (near_grid * near_cap + ranks(near_grid, owner_count)).reshape(-1)
    near_ask = spread(near_slot, src_row, owner_count * near_cap).reshape(owner_count, near_cap)
    near_got = lax.all_gather(to_all(near_ask), "batch", axis=0, tiled=True)
    near_count = jnp.sum((near_got > 0).astype(jnp.int32), axis=1)
    near_row = jnp.maximum(near_got - 1, 0).reshape(-1)

    same = (near_owner[:, None] == near_owner[None, :]) & (src_row[:, None] == src_row[None, :])
    places = jnp.arange(events, dtype=jnp.int32)
    pick = jnp.max(jnp.where(same, places[None, :], jnp.int32(-1)), axis=1, keepdims=True)
    source_code = cos_code((event_tick - source_tick).astype(F32), time_freq, time_phase)
    nb_code = cos_code((event_tick[None, :] - neighbour_tick.T).astype(F32), time_freq, time_phase)

    kv_rows, new_src, outgoing = update(
        slot, back, source_code, pick, near_slot[None, :], gru_input, gru_hidden, gru_bias[None, :],
        events, per_event, owner_count * near_cap,
    )
    arrived = to_all(outgoing.reshape(owner_count, near_cap, mem))
    fresh = lax.all_gather(arrived, "batch", axis=0, tiled=True).reshape(-1, mem)
    used = att + 2 * (mem + time) + att + mem
    embedding, packed = attend(
        kv_rows.reshape(per_event - 1, events, mem), nb_code, new_src, out_grad,
        w_query, w_kv, w_merge, merge_bias[None, :], used + 8, 256,
    )
    total = lax.psum(packed, ("node", "batch"))
    memory_out = write_back(near_row, near_count, fresh, memory, owner_count, batch_count, near_cap)
    kv_end = mem + 2 * (mem + time)
    grad_kv = jnp.concatenate([total[mem : mem + mem + time], total[mem + mem + time : kv_end]], axis=1)
    return embedding, memory_out, total[:mem], grad_kv, total[kv_end:used], total[used]


def solution(mesh):
    both = ("node", "batch")
    return jax.shard_map(
        on_device,
        mesh=mesh,
        in_specs=(
            P("node", None), P(both, None), P(both), P(both, None, None), P(both, None),
            P(both), P(both), P(both, None),
            P(), P(), P(), P(), P(), P(), P(), P(), P(),
            P(both, None),
        ),
        out_specs=(P(both, None), P("node", None), P(), P(), P(), P()),
        check_vma=False,
    )
```

```python
import functools
import math

import jax
import jax.numpy as jnp
from jax import lax
from jax.experimental import pallas as pl
from jax.experimental.pallas import tpu as pltpu
from jax.sharding import PartitionSpec as P

HEADS = 2
LANES = 128
F32 = jnp.float32
BF16 = jnp.bfloat16
VMEM = pltpu.VMEM
SMEM = pltpu.SMEM
COS_TERMS = [(-1.0) ** k * (2 * math.pi) ** (2 * k) / math.factorial(2 * k) for k in range(9)]


def cos_code(delta, freq, phase):
    turns = delta[..., None] * (freq * (0.5 / math.pi)) + phase * (0.5 / math.pi)
    turns = turns - jnp.round(turns)
    square = turns * turns
    total = jnp.full_like(square, COS_TERMS[-1])
    for term in COS_TERMS[-2::-1]:
        total = total * square + term
    return total.astype(BF16)


def ranks(owner_grid, owner_count):
    rows, lanes = owner_grid.shape
    masks = (owner_grid[None] == jnp.arange(owner_count, dtype=jnp.int32)[:, None, None]).astype(BF16)
    lane_before = jnp.triu(jnp.ones((lanes, lanes), BF16), 1)
    row_before = jnp.triu(jnp.ones((rows, rows), BF16), 1)
    within = jnp.einsum("orl,lm->orm", masks, lane_before, preferred_element_type=F32)
    totals = jnp.sum(masks.astype(F32), axis=-1).astype(BF16)
    base = jnp.einsum("or,rs->os", totals, row_before, preferred_element_type=F32)
    return jnp.sum(masks.astype(F32) * (within + base[:, :, None]), axis=0).astype(jnp.int32)


def spread(slot, value, slot_count):
    hi, lo = slot // LANES, slot % LANES
    bump = value + 1
    at_hi = hi[None, :] == jnp.arange(slot_count // LANES, dtype=jnp.int32)[:, None]
    upper = jnp.where(at_hi, (bump // 64).astype(F32)[None, :], 0.0).astype(BF16)
    lower = jnp.where(at_hi, (bump % 64).astype(F32)[None, :], 0.0).astype(BF16)
    at_lo = (lo[None, :] == jnp.arange(LANES, dtype=jnp.int32)[:, None]).astype(BF16)
    both = jnp.einsum(
        "he,le->hl", jnp.concatenate([upper, lower], 0), at_lo, preferred_element_type=F32
    ).astype(jnp.int32)
    half = slot_count // LANES
    return both[:half] * 64 + both[half:]


def widen(src_ref, dst_ref, step):
    @pl.loop(0, src_ref.shape[0] // step)
    def _(i):
        at = pl.ds(pl.multiple_of(i * step, step), step)
        dst_ref[at, :] = src_ref[at, :].astype(dst_ref.dtype)


def gather_kernel(owner_count, cap, index_ref, count_ref, table_ref, out_ref, wide, rows):
    widen(table_ref, wide, 256)

    @pl.loop(0, owner_count)
    def _(o):
        base = pl.multiple_of(o * cap, LANES)
        steps = (count_ref[o] + 15) // 16

        @pl.loop(0, steps)
        def _(i):
            for k in range(16):
                row = index_ref[base + i * 16 + k]
                rows[pl.ds(i * 16 + k, 1), :] = wide[pl.ds(row, 1), :]

        @pl.loop(0, steps)
        def _(i):
            at = pl.multiple_of(i * 16, 16)
            out_ref[pl.ds(pl.multiple_of(base + at, 16), 16), :] = rows[pl.ds(at, 16), :].astype(BF16)


def gather(index, count, table, owner_count, cap):
    return pl.pallas_call(
        functools.partial(gather_kernel, owner_count, cap),
        out_shape=jax.ShapeDtypeStruct((owner_count * cap, table.shape[1]), BF16),
        in_specs=[
            pl.BlockSpec(memory_space=SMEM),
            pl.BlockSpec(memory_space=SMEM),
            pl.BlockSpec(memory_space=VMEM),
        ],
        out_specs=pl.BlockSpec(memory_space=VMEM),
        scratch_shapes=[VMEM(table.shape, F32), VMEM((cap, table.shape[1]), F32)],
        compiler_params=pltpu.CompilerParams(vmem_limit_bytes=40 << 20),
        cost_estimate=pl.CostEstimate(flops=10**6, bytes_accessed=10**7, transcendentals=0),
    )(index, count, table)


def update_kernel(
    events, per_event, slot_ref, got_ref, code_ref, pick_ref, near_ref, gi_ref, gh_ref, bias_ref,
    rows_ref, new_ref, out_ref, wide, held,
):
    width = got_ref.shape[1]
    widen(got_ref, wide, 256)

    @pl.loop(0, slot_ref.shape[0] // 16)
    def _(i):
        for k in range(16):
            at = slot_ref[i * 16 + k]
            held[pl.ds(i * 16 + k, 1), :] = wide[pl.ds(at, 1), :]

    @pl.loop(0, events * (per_event - 1) // 256)
    def _(i):
        at = pl.ds(pl.multiple_of(events + i * 256, 256), 256)
        rows_ref[pl.ds(pl.multiple_of(i * 256, 256), 256), :] = held[at, :].astype(BF16)

    dest = held[:events, :].astype(BF16)
    wide_state = held[events * per_event :, :]
    dot = functools.partial(jnp.dot, preferred_element_type=F32)
    a = dot(dest, gi_ref[:width, :]) + dot(code_ref[...], gi_ref[width:, :]) + bias_ref[:, : 3 * width]
    b = dot(wide_state.astype(BF16), gh_ref[...])
    reset = jax.nn.sigmoid(a[:, :width] + b[:, :width])
    update = jax.nn.sigmoid(a[:, width : 2 * width] + b[:, width : 2 * width])
    cand = jnp.tanh(a[:, 2 * width :] + reset * (b[:, 2 * width :] + bias_ref[:, 3 * width :]))
    updated = ((1.0 - update) * cand + update * wide_state).astype(BF16)
    place = lax.broadcasted_iota(jnp.int32, (events, events), 1)
    chosen = (place == pick_ref[...]).astype(F32).astype(BF16)
    new_ref[...] = dot(chosen, updated).astype(BF16)
    slots = out_ref.shape[0]
    spot = lax.broadcasted_iota(jnp.int32, (slots, events), 0)
    out_ref[...] = dot((spot == near_ref[...]).astype(F32).astype(BF16), updated).astype(BF16)


def update(slot, got, code, pick, near_slot, gru_input, gru_hidden, bias, events, per_event, near_slots):
    width = got.shape[1]
    return pl.pallas_call(
        functools.partial(update_kernel, events, per_event),
        out_shape=(
            jax.ShapeDtypeStruct((events * (per_event - 1), width), BF16),
            jax.ShapeDtypeStruct((events, width), BF16),
            jax.ShapeDtypeStruct((near_slots, width), BF16),
        ),
        in_specs=[pl.BlockSpec(memory_space=SMEM)] + [pl.BlockSpec(memory_space=VMEM)] * 7,
        out_specs=(pl.BlockSpec(memory_space=VMEM),) * 3,
        scratch_shapes=[VMEM(got.shape, F32), VMEM((slot.shape[0], width), F32)],
        compiler_params=pltpu.CompilerParams(vmem_limit_bytes=48 << 20),
        cost_estimate=pl.CostEstimate(flops=10**6, bytes_accessed=10**7, transcendentals=0),
    )(slot, got, code, pick, near_slot, gru_input, gru_hidden, bias)


def attend_kernel(nb, rows_ref, code_ref, new_ref, grad_ref, wq_ref, wkv_ref, wm_ref, mb_ref, emb_ref, out_ref, kv, dkv):
    att = wq_ref.shape[1]
    mem = new_ref.shape[1]
    head = att // HEADS
    scale = 1.0 / math.sqrt(head)
    dot = functools.partial(jnp.dot, preferred_element_type=F32)
    same = (
        lax.broadcasted_iota(jnp.int32, (att, att), 0) // head
        == lax.broadcasted_iota(jnp.int32, (att, att), 1) // head
    ).astype(F32).astype(BF16)

    def head_sum(v):
        upper = v.astype(BF16)
        rest = (v - upper.astype(F32)).astype(BF16)
        return dot(upper, same) + dot(rest, same)

    def over_rows(x, y):
        return lax.dot_general(x, y, (((0,), (0,)), ((), ())), preferred_element_type=F32)

    new = new_ref[...]
    query = dot(new, wq_ref[...])
    scores = []
    for j in range(nb):
        kv[j] = dot(rows_ref[j], wkv_ref[:mem, :]) + dot(code_ref[j], wkv_ref[mem:, :])
        scores.append(head_sum(query * kv[j, :, :att]) * scale)
    top = functools.reduce(jnp.maximum, scores)
    shares = [jnp.exp(s - top) for s in scores]
    inverse = 1.0 / functools.reduce(jnp.add, shares)
    shares = [s * inverse for s in shares]
    mixed = functools.reduce(jnp.add, [shares[j] * kv[j, :, att:] for j in range(nb)]).astype(BF16)
    z = dot(mixed, wm_ref[:att, :]) + dot(new, wm_ref[att:, :]) + mb_ref[...]
    gate = 1.0 / (1.0 + jnp.exp(-z))
    emb_ref[...] = z * gate
    dz = grad_ref[...] * (gate * (1.0 + z * (1.0 - gate)))
    dz16 = dz.astype(BF16)
    dmixed = lax.dot_general(
        dz16, wm_ref[:att, :], (((1,), (1,)), ((), ())), preferred_element_type=F32
    ).astype(BF16).astype(F32)
    dshare = [head_sum(dmixed * kv[j, :, att:]) for j in range(nb)]
    mean = functools.reduce(jnp.add, [shares[j] * dshare[j] for j in range(nb)])
    dquery = jnp.zeros_like(query)
    for j in range(nb):
        dscore = shares[j] * (dshare[j] - mean) * scale
        dquery += dscore * kv[j, :, :att]
        dkv[j, :, :att] = (dscore * query).astype(BF16)
        dkv[j, :, att:] = (shares[j] * dmixed).astype(BF16)
    flat = dkv[...].reshape(-1, 2 * att)
    from_row = over_rows(rows_ref[...].reshape(-1, mem), flat)
    from_code = over_rows(code_ref[...].reshape(-1, code_ref.shape[2]), flat)

    @pl.when(pl.program_id(0) == 0)
    def _():
        out_ref[...] = jnp.zeros_like(out_ref)

    at = 0
    for piece in (
        over_rows(new, dquery.astype(BF16)),
        from_row[:, :att],
        from_code[:, :att],
        from_row[:, att:],
        from_code[:, att:],
        over_rows(mixed, dz16),
        over_rows(new, dz16),
    ):
        out_ref[at : at + piece.shape[0], :] += piece
        at += piece.shape[0]
    out_ref[at : at + 1, :] += jnp.sum(dz, axis=0, keepdims=True)


def attend(rows, code, new, out_grad, wq, wkv, wm, mb, packed_rows, block):
    nb, events, mem = rows.shape
    time = code.shape[2]
    att = wq.shape[1]
    whole = lambda a: pl.BlockSpec(a.shape, lambda i: (0,) * a.ndim)
    return pl.pallas_call(
        functools.partial(attend_kernel, nb),
        grid=(events // block,),
        out_shape=(
            jax.ShapeDtypeStruct(out_grad.shape, F32),
            jax.ShapeDtypeStruct((packed_rows, LANES), F32),
        ),
        in_specs=[
            pl.BlockSpec((nb, block, mem), lambda i: (0, i, 0)),
            pl.BlockSpec((nb, block, time), lambda i: (0, i, 0)),
            pl.BlockSpec((block, mem), lambda i: (i, 0)),
            pl.BlockSpec((block, mem), lambda i: (i, 0)),
            whole(wq),
            whole(wkv),
            whole(wm),
            whole(mb),
        ],
        out_specs=(
            pl.BlockSpec((block, mem), lambda i: (i, 0)),
            pl.BlockSpec((packed_rows, LANES), lambda i: (0, 0)),
        ),
        scratch_shapes=[VMEM((nb, block, 2 * att), F32), VMEM((nb, block, 2 * att), BF16)],
        compiler_params=pltpu.CompilerParams(vmem_limit_bytes=48 << 20),
        cost_estimate=pl.CostEstimate(flops=3 * 10**9, bytes_accessed=10**7, transcendentals=10**6),
    )(rows, code, new, out_grad, wq, wkv, wm, mb)


def write_kernel(senders, batches, cap, row_ref, count_ref, fresh_ref, table_ref, out_ref, wide, rows):
    widen(table_ref, wide, 256)
    widen(fresh_ref, rows, 256)

    @pl.loop(0, senders * batches)
    def _(order):
        block = lax.rem(order, batches) * senders + lax.div(order, batches)
        base = block * cap
        count = count_ref[block]

        @pl.loop(0, lax.div(count, 8))
        def _(i):
            for k in range(8):
                at = base + i * 8 + k
                wide[pl.ds(row_ref[at], 1), :] = rows[pl.ds(at, 1), :]

        @pl.loop(lax.div(count, 8) * 8, count)
        def _(i):
            wide[pl.ds(row_ref[base + i], 1), :] = rows[pl.ds(base + i, 1), :]

    widen(wide, out_ref, 256)


def write_back(row, count, fresh, table, senders, batches, cap):
    return pl.pallas_call(
        functools.partial(write_kernel, senders, batches, cap),
        out_shape=jax.ShapeDtypeStruct(table.shape, BF16),
        in_specs=[
            pl.BlockSpec(memory_space=SMEM),
            pl.BlockSpec(memory_space=SMEM),
            pl.BlockSpec(memory_space=VMEM),
            pl.BlockSpec(memory_space=VMEM),
        ],
        out_specs=pl.BlockSpec(memory_space=VMEM),
        scratch_shapes=[VMEM(table.shape, F32), VMEM(fresh.shape, F32)],
        compiler_params=pltpu.CompilerParams(vmem_limit_bytes=40 << 20),
        cost_estimate=pl.CostEstimate(flops=10**6, bytes_accessed=10**7, transcendentals=0),
    )(row, count, fresh, table)


def on_device(
    memory, src_owner, src_row, fetch_owner, fetch_row, event_tick, source_tick, neighbour_tick,
    time_freq, time_phase, gru_input, gru_hidden, gru_bias, w_query, w_kv, w_merge, merge_bias, out_grad,
):
    owner_count = lax.axis_size("node")
    batch_count = lax.axis_size("batch")
    events = src_row.shape[0]
    per_event = fetch_row.shape[1]
    mem = memory.shape[1]
    att = w_query.shape[1]
    time = time_freq.shape[0]
    near_cap = events * 2 // owner_count
    cap = near_cap * (per_event + 1)
    to_all = functools.partial(lax.all_to_all, axis_name="node", split_axis=0, concat_axis=0, tiled=True)

    near_owner = src_owner[:, 0]
    owners = jnp.concatenate([fetch_owner[:, :, 0].T, near_owner[None]], 0).reshape(-1, LANES)
    wanted = jnp.concatenate([fetch_row.T, src_row[None]], 0).reshape(-1)
    slot = (owners * cap + ranks(owners, owner_count)).reshape(-1)
    ask = spread(slot, wanted, owner_count * cap).reshape(owner_count, cap)
    near_grid = near_owner.reshape(-1, LANES)
    near_slot = (near_grid * near_cap + ranks(near_grid, owner_count)).reshape(-1)
    near_ask = spread(near_slot, src_row, owner_count * near_cap).reshape(owner_count, near_cap)
    asked = to_all(jnp.concatenate([ask, near_ask], axis=1))
    got = asked[:, :cap]
    count = jnp.sum((got > 0).astype(jnp.int32), axis=1)
    index = jnp.maximum(got - 1, 0).reshape(-1)
    sent = gather(index, count, memory, owner_count, cap)
    back = to_all(sent.reshape(owner_count, cap, mem)).reshape(-1, mem)

    near_got = lax.all_gather(asked[:, cap:], "batch", axis=0, tiled=True)
    near_count = jnp.sum((near_got > 0).astype(jnp.int32), axis=1)
    near_row = jnp.maximum(near_got - 1, 0).reshape(-1)

    same = (near_owner[:, None] == near_owner[None, :]) & (src_row[:, None] == src_row[None, :])
    places = jnp.arange(events, dtype=jnp.int32)
    pick = jnp.max(jnp.where(same, places[None, :], jnp.int32(-1)), axis=1, keepdims=True)
    source_code = cos_code((event_tick - source_tick).astype(F32), time_freq, time_phase)
    nb_code = cos_code((event_tick[None, :] - neighbour_tick.T).astype(F32), time_freq, time_phase)

    kv_rows, new_src, outgoing = update(
        slot, back, source_code, pick, near_slot[None, :], gru_input, gru_hidden, gru_bias[None, :],
        events, per_event, owner_count * near_cap,
    )
    arrived = to_all(outgoing.reshape(owner_count, near_cap, mem))
    fresh = lax.all_gather(arrived, "batch", axis=0, tiled=True).reshape(-1, mem)
    used = att + 2 * (mem + time) + att + mem
    devices = owner_count * batch_count
    packed_rows = -(-(used + 1) // (8 * devices)) * 8 * devices
    embedding, packed = attend(
        kv_rows.reshape(per_event - 1, events, mem), nb_code, new_src, out_grad,
        w_query, w_kv, w_merge, merge_bias[None, :], packed_rows, 256,
    )
    both = ("node", "batch")
    parts = lax.all_to_all(packed.reshape(devices, -1, LANES), both, split_axis=0, concat_axis=0, tiled=True)
    total = lax.all_gather(jnp.sum(parts, axis=0), both, axis=0, tiled=True)
    memory_out = write_back(near_row, near_count, fresh, memory, owner_count, batch_count, near_cap)
    kv_end = mem + 2 * (mem + time)
    grad_kv = jnp.concatenate([total[mem : mem + mem + time], total[mem + mem + time : kv_end]], axis=1)
    return embedding, memory_out, total[:mem], grad_kv, total[kv_end:used], total[used]


def solution(mesh):
    both = ("node", "batch")
    return jax.shard_map(
        on_device,
        mesh=mesh,
        in_specs=(
            P("node", None), P(both, None), P(both), P(both, None, None), P(both, None),
            P(both), P(both), P(both, None),
            P(), P(), P(), P(), P(), P(), P(), P(), P(),
            P(both, None),
        ),
        out_specs=(P(both, None), P("node", None), P(), P(), P(), P()),
        check_vma=False,
    )
```

```python
import functools
import math

import jax
import jax.numpy as jnp
from jax import lax
from jax.experimental import pallas as pl
from jax.experimental.pallas import tpu as pltpu
from jax.sharding import PartitionSpec as P

HEADS = 2
LANES = 128
F32 = jnp.float32
BF16 = jnp.bfloat16
VMEM = pltpu.VMEM
SMEM = pltpu.SMEM
COS_TERMS = [(-1.0) ** k * (2 * math.pi) ** (2 * k) / math.factorial(2 * k) for k in range(9)]


def cos_code(delta, freq, phase):
    turns = delta[..., None] * (freq * (0.5 / math.pi)) + phase * (0.5 / math.pi)
    turns = turns - jnp.round(turns)
    square = turns * turns
    total = jnp.full_like(square, COS_TERMS[-1])
    for term in COS_TERMS[-2::-1]:
        total = total * square + term
    return total.astype(BF16)


def ranks(owner_grid, owner_count):
    rows, lanes = owner_grid.shape
    masks = (owner_grid[None] == jnp.arange(owner_count, dtype=jnp.int32)[:, None, None]).astype(BF16)
    lane_before = jnp.triu(jnp.ones((lanes, lanes), BF16), 1)
    row_before = jnp.triu(jnp.ones((rows, rows), BF16), 1)
    within = jnp.einsum("orl,lm->orm", masks, lane_before, preferred_element_type=F32)
    totals = jnp.sum(masks.astype(F32), axis=-1).astype(BF16)
    base = jnp.einsum("or,rs->os", totals, row_before, preferred_element_type=F32)
    return jnp.sum(masks.astype(F32) * (within + base[:, :, None]), axis=0).astype(jnp.int32)


def spread(slot, value, slot_count):
    hi, lo = slot // LANES, slot % LANES
    bump = value + 1
    at_hi = hi[None, :] == jnp.arange(slot_count // LANES, dtype=jnp.int32)[:, None]
    upper = jnp.where(at_hi, (bump // 64).astype(F32)[None, :], 0.0).astype(BF16)
    lower = jnp.where(at_hi, (bump % 64).astype(F32)[None, :], 0.0).astype(BF16)
    at_lo = (lo[None, :] == jnp.arange(LANES, dtype=jnp.int32)[:, None]).astype(BF16)
    both = jnp.einsum(
        "he,le->hl", jnp.concatenate([upper, lower], 0), at_lo, preferred_element_type=F32
    ).astype(jnp.int32)
    half = slot_count // LANES
    return both[:half] * 64 + both[half:]


def widen(src_ref, dst_ref, step):
    @pl.loop(0, src_ref.shape[0] // step)
    def _(i):
        at = pl.ds(pl.multiple_of(i * step, step), step)
        dst_ref[at, :] = src_ref[at, :].astype(dst_ref.dtype)


def gather_kernel(owner_count, cap, index_ref, count_ref, table_ref, out_ref, wide, rows):
    widen(table_ref, wide, 256)

    @pl.loop(0, owner_count)
    def _(o):
        base = pl.multiple_of(o * cap, LANES)
        steps = (count_ref[o] + 15) // 16

        @pl.loop(0, steps)
        def _(i):
            for k in range(16):
                row = index_ref[base + i * 16 + k]
                rows[pl.ds(i * 16 + k, 1), :] = wide[pl.ds(row, 1), :]

        @pl.loop(0, steps)
        def _(i):
            at = pl.multiple_of(i * 16, 16)
            out_ref[pl.ds(pl.multiple_of(base + at, 16), 16), :] = rows[pl.ds(at, 16), :].astype(BF16)


def gather(index, count, table, owner_count, cap):
    return pl.pallas_call(
        functools.partial(gather_kernel, owner_count, cap),
        out_shape=jax.ShapeDtypeStruct((owner_count * cap, table.shape[1]), BF16),
        in_specs=[
            pl.BlockSpec(memory_space=SMEM),
            pl.BlockSpec(memory_space=SMEM),
            pl.BlockSpec(memory_space=VMEM),
        ],
        out_specs=pl.BlockSpec(memory_space=VMEM),
        scratch_shapes=[VMEM(table.shape, F32), VMEM((cap, table.shape[1]), F32)],
        compiler_params=pltpu.CompilerParams(vmem_limit_bytes=40 << 20),
        cost_estimate=pl.CostEstimate(flops=10**6, bytes_accessed=10**7, transcendentals=0),
    )(index, count, table)


def update_kernel(
    events, per_event, slot_ref, got_ref, code_ref, pick_ref, near_ref, gi_ref, gh_ref, bias_ref,
    rows_ref, new_ref, out_ref, wide, held,
):
    width = got_ref.shape[1]
    widen(got_ref, wide, 256)

    @pl.loop(0, slot_ref.shape[0] // 16)
    def _(i):
        for k in range(16):
            at = slot_ref[i * 16 + k]
            held[pl.ds(i * 16 + k, 1), :] = wide[pl.ds(at, 1), :]

    @pl.loop(0, events * (per_event - 1) // 256)
    def _(i):
        at = pl.ds(pl.multiple_of(events + i * 256, 256), 256)
        rows_ref[pl.ds(pl.multiple_of(i * 256, 256), 256), :] = held[at, :].astype(BF16)

    dest = held[:events, :].astype(BF16)
    wide_state = held[events * per_event :, :]
    dot = functools.partial(jnp.dot, preferred_element_type=F32)
    a = dot(dest, gi_ref[:width, :]) + dot(code_ref[...], gi_ref[width:, :]) + bias_ref[:, : 3 * width]
    b = dot(wide_state.astype(BF16), gh_ref[...])
    reset = jax.nn.sigmoid(a[:, :width] + b[:, :width])
    update = jax.nn.sigmoid(a[:, width : 2 * width] + b[:, width : 2 * width])
    cand = jnp.tanh(a[:, 2 * width :] + reset * (b[:, 2 * width :] + bias_ref[:, 3 * width :]))
    updated = ((1.0 - update) * cand + update * wide_state).astype(BF16)
    place = lax.broadcasted_iota(jnp.int32, (events, events), 1)
    chosen = (place == pick_ref[...]).astype(F32).astype(BF16)
    new_ref[...] = dot(chosen, updated).astype(BF16)
    slots = out_ref.shape[0]
    spot = lax.broadcasted_iota(jnp.int32, (slots, events), 0)
    out_ref[...] = dot((spot == near_ref[...]).astype(F32).astype(BF16), updated).astype(BF16)


def update(slot, got, code, pick, near_slot, gru_input, gru_hidden, bias, events, per_event, near_slots):
    width = got.shape[1]
    return pl.pallas_call(
        functools.partial(update_kernel, events, per_event),
        out_shape=(
            jax.ShapeDtypeStruct((events * (per_event - 1), width), BF16),
            jax.ShapeDtypeStruct((events, width), BF16),
            jax.ShapeDtypeStruct((near_slots, width), BF16),
        ),
        in_specs=[pl.BlockSpec(memory_space=SMEM)] + [pl.BlockSpec(memory_space=VMEM)] * 7,
        out_specs=(pl.BlockSpec(memory_space=VMEM),) * 3,
        scratch_shapes=[VMEM(got.shape, F32), VMEM((slot.shape[0], width), F32)],
        compiler_params=pltpu.CompilerParams(vmem_limit_bytes=48 << 20),
        cost_estimate=pl.CostEstimate(flops=10**6, bytes_accessed=10**7, transcendentals=0),
    )(slot, got, code, pick, near_slot, gru_input, gru_hidden, bias)


def attend_kernel(nb, rows_ref, code_ref, new_ref, grad_ref, wq_ref, wkv_ref, wm_ref, mb_ref, emb_ref, out_ref, kv, dkv):
    att = wq_ref.shape[1]
    mem = new_ref.shape[1]
    head = att // HEADS
    scale = 1.0 / math.sqrt(head)
    dot = functools.partial(jnp.dot, preferred_element_type=F32)
    same = (
        lax.broadcasted_iota(jnp.int32, (att, att), 0) // head
        == lax.broadcasted_iota(jnp.int32, (att, att), 1) // head
    ).astype(F32).astype(BF16)

    def head_sum(v):
        upper = v.astype(BF16)
        rest = (v - upper.astype(F32)).astype(BF16)
        return dot(upper, same) + dot(rest, same)

    def over_rows(x, y):
        return lax.dot_general(x, y, (((0,), (0,)), ((), ())), preferred_element_type=F32)

    new = new_ref[...]
    query = dot(new, wq_ref[...])
    scores = []
    for j in range(nb):
        kv[j] = dot(rows_ref[j], wkv_ref[:mem, :]) + dot(code_ref[j], wkv_ref[mem:, :])
        scores.append(head_sum(query * kv[j, :, :att]) * scale)
    top = functools.reduce(jnp.maximum, scores)
    shares = [jnp.exp(s - top) for s in scores]
    inverse = 1.0 / functools.reduce(jnp.add, shares)
    shares = [s * inverse for s in shares]
    mixed = functools.reduce(jnp.add, [shares[j] * kv[j, :, att:] for j in range(nb)]).astype(BF16)
    z = dot(mixed, wm_ref[:att, :]) + dot(new, wm_ref[att:, :]) + mb_ref[...]
    gate = 1.0 / (1.0 + jnp.exp(-z))
    emb_ref[...] = z * gate
    dz = grad_ref[...] * (gate * (1.0 + z * (1.0 - gate)))
    dz16 = dz.astype(BF16)
    dmixed = lax.dot_general(
        dz16, wm_ref[:att, :], (((1,), (1,)), ((), ())), preferred_element_type=F32
    ).astype(BF16).astype(F32)
    dshare = [head_sum(dmixed * kv[j, :, att:]) for j in range(nb)]
    mean = functools.reduce(jnp.add, [shares[j] * dshare[j] for j in range(nb)])
    dquery = jnp.zeros_like(query)
    for j in range(nb):
        dscore = shares[j] * (dshare[j] - mean) * scale
        dquery += dscore * kv[j, :, :att]
        dkv[j, :, :att] = (dscore * query).astype(BF16)
        dkv[j, :, att:] = (shares[j] * dmixed).astype(BF16)
    flat = dkv[...].reshape(-1, 2 * att)
    from_row = over_rows(rows_ref[...].reshape(-1, mem), flat)
    from_code = over_rows(code_ref[...].reshape(-1, code_ref.shape[2]), flat)

    @pl.when(pl.program_id(0) == 0)
    def _():
        out_ref[...] = jnp.zeros_like(out_ref)

    at = 0
    for piece in (
        over_rows(new, dquery.astype(BF16)),
        from_row[:, :att],
        from_code[:, :att],
        from_row[:, att:],
        from_code[:, att:],
        over_rows(mixed, dz16),
        over_rows(new, dz16),
    ):
        out_ref[at : at + piece.shape[0], :] += piece
        at += piece.shape[0]
    out_ref[at : at + 1, :] += jnp.sum(dz, axis=0, keepdims=True)


def attend(rows, code, new, out_grad, wq, wkv, wm, mb, packed_rows, block):
    nb, events, mem = rows.shape
    time = code.shape[2]
    att = wq.shape[1]
    whole = lambda a: pl.BlockSpec(a.shape, lambda i: (0,) * a.ndim)
    return pl.pallas_call(
        functools.partial(attend_kernel, nb),
        grid=(events // block,),
        out_shape=(
            jax.ShapeDtypeStruct(out_grad.shape, F32),
            jax.ShapeDtypeStruct((packed_rows, LANES), F32),
        ),
        in_specs=[
            pl.BlockSpec((nb, block, mem), lambda i: (0, i, 0)),
            pl.BlockSpec((nb, block, time), lambda i: (0, i, 0)),
            pl.BlockSpec((block, mem), lambda i: (i, 0)),
            pl.BlockSpec((block, mem), lambda i: (i, 0)),
            whole(wq),
            whole(wkv),
            whole(wm),
            whole(mb),
        ],
        out_specs=(
            pl.BlockSpec((block, mem), lambda i: (i, 0)),
            pl.BlockSpec((packed_rows, LANES), lambda i: (0, 0)),
        ),
        scratch_shapes=[VMEM((nb, block, 2 * att), F32), VMEM((nb, block, 2 * att), BF16)],
        compiler_params=pltpu.CompilerParams(vmem_limit_bytes=48 << 20),
        cost_estimate=pl.CostEstimate(flops=3 * 10**9, bytes_accessed=10**7, transcendentals=10**6),
    )(rows, code, new, out_grad, wq, wkv, wm, mb)


def write_kernel(senders, batches, cap, row_ref, count_ref, fresh_ref, table_ref, out_ref, wide, rows):
    widen(table_ref, wide, 256)
    widen(fresh_ref, rows, 256)

    @pl.loop(0, senders * batches)
    def _(order):
        block = lax.rem(order, batches) * senders + lax.div(order, batches)
        base = block * cap
        count = count_ref[block]

        @pl.loop(0, lax.div(count, 8))
        def _(i):
            for k in range(8):
                at = base + i * 8 + k
                wide[pl.ds(row_ref[at], 1), :] = rows[pl.ds(at, 1), :]

        @pl.loop(lax.div(count, 8) * 8, count)
        def _(i):
            wide[pl.ds(row_ref[base + i], 1), :] = rows[pl.ds(base + i, 1), :]

    widen(wide, out_ref, 256)


def write_back(row, count, fresh, table, senders, batches, cap):
    return pl.pallas_call(
        functools.partial(write_kernel, senders, batches, cap),
        out_shape=jax.ShapeDtypeStruct(table.shape, BF16),
        in_specs=[
            pl.BlockSpec(memory_space=SMEM),
            pl.BlockSpec(memory_space=SMEM),
            pl.BlockSpec(memory_space=VMEM),
            pl.BlockSpec(memory_space=VMEM),
        ],
        out_specs=pl.BlockSpec(memory_space=VMEM),
        scratch_shapes=[VMEM(table.shape, F32), VMEM(fresh.shape, F32)],
        compiler_params=pltpu.CompilerParams(vmem_limit_bytes=40 << 20),
        cost_estimate=pl.CostEstimate(flops=10**6, bytes_accessed=10**7, transcendentals=0),
    )(row, count, fresh, table)


def on_device(
    memory, src_owner, src_row, fetch_owner, fetch_row, event_tick, source_tick, neighbour_tick,
    time_freq, time_phase, gru_input, gru_hidden, gru_bias, w_query, w_kv, w_merge, merge_bias, out_grad,
):
    owner_count = lax.axis_size("node")
    batch_count = lax.axis_size("batch")
    events = src_row.shape[0]
    per_event = fetch_row.shape[1]
    mem = memory.shape[1]
    att = w_query.shape[1]
    time = time_freq.shape[0]
    near_cap = events * 2 // owner_count
    cap = near_cap * (per_event + 1)
    to_all = functools.partial(lax.all_to_all, axis_name="node", split_axis=0, concat_axis=0, tiled=True)

    near_owner = src_owner[:, 0]
    owners = jnp.concatenate([fetch_owner[:, :, 0].T, near_owner[None]], 0).reshape(-1, LANES)
    wanted = jnp.concatenate([fetch_row.T, src_row[None]], 0).reshape(-1)
    slot = (owners * cap + ranks(owners, owner_count)).reshape(-1)
    ask = spread(slot, wanted, owner_count * cap).reshape(owner_count, cap)
    near_grid = near_owner.reshape(-1, LANES)
    near_slot = (near_grid * near_cap + ranks(near_grid, owner_count)).reshape(-1)
    near_ask = spread(near_slot, src_row, owner_count * near_cap).reshape(owner_count, near_cap)
    asked = to_all(jnp.concatenate([ask, near_ask], axis=1))
    got = asked[:, :cap]
    count = jnp.sum((got > 0).astype(jnp.int32), axis=1)
    index = jnp.maximum(got - 1, 0).reshape(-1)
    sent = gather(index, count, memory, owner_count, cap)
    back = to_all(sent.reshape(owner_count, cap, mem)).reshape(-1, mem)

    near_got = lax.all_gather(asked[:, cap:], "batch", axis=0, tiled=True)
    near_count = jnp.sum((near_got > 0).astype(jnp.int32), axis=1)
    near_row = jnp.maximum(near_got - 1, 0).reshape(-1)

    same = (near_owner[:, None] == near_owner[None, :]) & (src_row[:, None] == src_row[None, :])
    places = jnp.arange(events, dtype=jnp.int32)
    pick = jnp.max(jnp.where(same, places[None, :], jnp.int32(-1)), axis=1, keepdims=True)
    source_code = cos_code((event_tick - source_tick).astype(F32), time_freq, time_phase)
    nb_code = cos_code((event_tick[None, :] - neighbour_tick.T).astype(F32), time_freq, time_phase)

    kv_rows, new_src, outgoing = update(
        slot, back, source_code, pick, near_slot[None, :], gru_input, gru_hidden, gru_bias[None, :],
        events, per_event, owner_count * near_cap,
    )
    arrived = to_all(outgoing.reshape(owner_count, near_cap, mem))
    fresh = lax.all_gather(arrived, "batch", axis=0, tiled=True).reshape(-1, mem)
    used = att + 2 * (mem + time) + att + mem
    devices = owner_count * batch_count
    packed_rows = -(-(used + 1) // (8 * devices)) * 8 * devices
    embedding, packed = attend(
        kv_rows.reshape(per_event - 1, events, mem), nb_code, new_src, out_grad,
        w_query, w_kv, w_merge, merge_bias[None, :], packed_rows, 256,
    )
    both = ("node", "batch")
    parts = lax.all_to_all(packed.reshape(devices, -1, LANES), both, split_axis=0, concat_axis=0, tiled=True)
    share = jnp.broadcast_to(jnp.sum(parts, axis=0)[None], parts.shape)
    total = lax.all_to_all(share, both, split_axis=0, concat_axis=0, tiled=True).reshape(-1, LANES)
    memory_out = write_back(near_row, near_count, fresh, memory, owner_count, batch_count, near_cap)
    kv_end = mem + 2 * (mem + time)
    grad_kv = jnp.concatenate([total[mem : mem + mem + time], total[mem + mem + time : kv_end]], axis=1)
    return embedding, memory_out, total[:mem], grad_kv, total[kv_end:used], total[used]


def solution(mesh):
    both = ("node", "batch")
    return jax.shard_map(
        on_device,
        mesh=mesh,
        in_specs=(
            P("node", None), P(both, None), P(both), P(both, None, None), P(both, None),
            P(both), P(both), P(both, None),
            P(), P(), P(), P(), P(), P(), P(), P(), P(),
            P(both, None),
        ),
        out_specs=(P(both, None), P("node", None), P(), P(), P(), P()),
        check_vma=False,
    )
```
